32 devices in a mesh: tm: 4 (over y, x), head: 8 (over z, core).
Axes of the slice: x: 2, y: 2, z: 4, core: 2. Of those that a mesh axis runs over, the one named last changes fastest.
Arguments:
- queries: bfloat16 [8192, 4096], P('tm', 'head'), may hold values from -64 to 64
- saved_keys: bfloat16 [8192, 4096], P('tm', 'head'), may hold values from -16 to 16
- saved_values: bfloat16 [8192, 4096], P('tm', 'head'), may hold values from -6 to 6
- out_grad: bfloat16 [8192, 4096], P(('tm', 'head')), may hold values from -6 to 6
- radius: int32 [32], P('head'), may hold values from 0 to 2, as said below
- clip_ids: int32 [32], replicated, may hold values from 0 to 4, never falling along the last dimension, each value on 1 to 12 neighbouring positions
Outputs:
- grad_queries: bfloat16 [8192, 4096], P('tm', 'head')
- grad_keys: bfloat16 [8192, 4096], P('tm', 'head')
- grad_values: bfloat16 [8192, 4096], P('tm', 'head')
The draws below stay inside these ranges and needn't reach their ends.
Inputs may be any that keep to these rules, and one draw needn't show every extreme that they name: Some head has radius exactly 2 and some head radius 0.
All inputs are finite; a program needn't handle non-finite values.
Results may differ from the reference program's by a relative error of at most 0.012.
Values may be sent and summed in bfloat16 or wider, within the bound.
A program may use at most 256 MiB of HBM per device.

```python
import math
import jax
import jax.numpy as jnp
import numpy as np
from jax import lax

HEADS = 32
HD = 128
FRAME = 256
RADIUS = 2
D = 4096
FRAMES = 32
TOKENS = 8192


def draw_pair(key):
    base_key = jax.random.fold_in(key, 11)
    key_rows = jax.random.normal(jax.random.fold_in(base_key, 1), (TOKENS, HEADS, HD), jnp.float32)
    query_rows = jax.random.normal(jax.random.fold_in(base_key, 2), (TOKENS, HEADS, HD), jnp.float32)
    query_rows = jnp.clip(query_rows, -6.0, 6.0)
    key_rows = jnp.clip(key_rows, -6.0, 6.0)
    return (query_rows.reshape(TOKENS, HEADS * HD).astype(jnp.bfloat16), key_rows.reshape(TOKENS, HEADS * HD).astype(jnp.bfloat16))


def draw_queries(key, part):
    return draw_pair(key)[0]


def draw_saved_keys(key, part):
    return draw_pair(key)[1]


def draw_radius(key, part):
    values = jax.random.randint(key, (HEADS,), 0, RADIUS + 1, jnp.int32)
    chosen = jax.random.randint(jax.random.fold_in(key, 1), (), 0, HEADS, jnp.int32)
    other = (chosen + 1 + jax.random.randint(jax.random.fold_in(key, 2), (), 0, HEADS - 1, jnp.int32)) % HEADS
    values = values.at[chosen].set(RADIUS)
    values = values.at[other].set(0)
    return values.astype(jnp.int32)


def levels(stream_key, shape, pieces, low, high):
    level = 1.0
    for position, parts in pieces:
        steps = jax.random.uniform(jax.random.fold_in(jax.random.fold_in(stream_key, 6), position), (parts,), jnp.float32, low / len(pieces), high / len(pieces))
        level = level * jnp.repeat(jnp.exp(steps), shape[position] // parts).reshape((-1,) + (1,) * (len(shape) - 1 - position))
    return level


def profile(amount, total, reach, slope):
    portions = [(1 << 20) // math.isqrt(standing ** slope) + 1 for standing in range(2, amount + 1)]
    spare, given = total - reach - (amount - 1), [1] * (amount - 1)
    while spare > 0:
        candidates = [i for i in range(amount - 1) if given[i] < reach]
        whole, remaining = sum([portions[i] for i in candidates]), spare
        for i in candidates:
            more = min(reach - given[i], max(1, remaining * portions[i] // whole), spare)
            given[i] = given[i] + more
            spare = spare - more
    return np.array([reach] + given)


def uneven_parts(stream_key, number_of, total, reach, slope):
    if number_of == 2:
        one = jax.random.randint(stream_key, (), max(1, total - reach), min(reach, total - 1) + 1)
        return jnp.stack([one, total - one])
    sizes = jnp.asarray(profile(number_of, total, reach, slope), jnp.int32)
    pairs = (number_of - 1) // 2
    giver, sink = sizes[1:1 + 2 * pairs:2], sizes[2:2 + 2 * pairs:2]
    margin = jnp.minimum(giver - 1, reach - sink)
    shifted = jax.random.randint(jax.random.fold_in(stream_key, 1), (pairs,), 0, 1 << 20) % (margin + 1)
    sizes = sizes.at[1:1 + 2 * pairs:2].set(giver - shifted).at[2:2 + 2 * pairs:2].set(sink + shifted)
    return sizes[jax.random.permutation(jax.random.fold_in(stream_key, 2), number_of)]


def centred(own_key, dims, scale, most, cuts=(), kind=jnp.bfloat16):
    factor_of = levels(own_key, dims, cuts, -0.22, 0.18) if cuts else 1.0
    values = jax.random.normal(own_key, dims, jnp.float32) * scale * factor_of
    return jnp.minimum(jnp.maximum(values, -most), most).astype(kind)


def setup_inputs(seed: int = 0) -> dict:
    key_of = jax.random.split(jax.random.key(seed), 7)
    queries = draw_queries(jax.random.fold_in(key_of[6], 71), 0)
    saved_keys = draw_saved_keys(jax.random.fold_in(key_of[6], 71), 0)
    saved_values = centred(key_of[2], (TOKENS, D), 1.0, 6.0, ((0, 4), (1, 8)))
    out_grad = centred(key_of[3], (TOKENS, D), 1.0, 6.0, ((0, 32),))
    radius = draw_radius(jax.random.fold_in(key_of[6], 71), 0)
    clip_ids = jnp.searchsorted(jnp.cumsum(uneven_parts(key_of[5], FRAMES // 6, FRAMES, 12, 0)), jnp.arange(FRAMES), side="right").astype(jnp.int32)
    return dict(queries=queries, saved_keys=saved_keys, saved_values=saved_values, out_grad=out_grad, radius=radius, clip_ids=clip_ids)


def reference(queries, saved_keys, saved_values, out_grad, radius, clip_ids):
    span = 2 * RADIUS + 1
    scale = HD ** -0.5

    def one_head(head_index):
        start = (head_index * HD).astype(jnp.int32)

        def columns(whole):
            return lax.dynamic_slice_in_dim(whole, start, HD, 1).astype(jnp.float32).reshape(FRAMES, FRAME, HD)

        query_part = columns(queries)
        key_part = columns(saved_keys)
        value_part = columns(saved_values)
        grad_part = columns(out_grad)
        padding = ((RADIUS, RADIUS), (0, 0), (0, 0))
        key_padded = jnp.pad(key_part, padding)
        value_padded = jnp.pad(value_part, padding)
        key_window = jnp.stack([key_padded[offset:offset + FRAMES] for offset in range(span)], 1)
        value_window = jnp.stack([value_padded[offset:offset + FRAMES] for offset in range(span)], 1)
        frame_index = jnp.arange(FRAMES, dtype=jnp.int32)
        steps_away = jnp.arange(span, dtype=jnp.int32) - RADIUS
        key_frame = frame_index[:, None] + steps_away[None, :]
        inside = (key_frame >= 0) & (key_frame < FRAMES)
        key_clip = clip_ids[jnp.clip(key_frame, 0, FRAMES - 1)]
        within = jnp.abs(steps_away) <= radius[head_index]
        valid = inside & (clip_ids[:, None] == key_clip) & within[None, :]
        scores = jnp.einsum('aqd,ajkd->aqjk', query_part, key_window) * scale
        scores = jnp.where(valid[:, None, :, None], scores, -1e30)
        highest = jnp.max(scores, axis=(2, 3), keepdims=True)
        expo = jnp.exp(scores - highest)
        probs = expo / jnp.sum(expo, axis=(2, 3), keepdims=True)
        probs_b = probs.astype(jnp.bfloat16).astype(jnp.float32)
        dprobs = jnp.einsum('aqd,ajkd->aqjk', grad_part, value_window)
        delta = jnp.sum(probs * dprobs, axis=(2, 3), keepdims=True)
        dscores = (probs * (dprobs - delta)).astype(jnp.bfloat16).astype(jnp.float32)
        grad_query = jnp.einsum('aqjk,ajkd->aqd', dscores, key_window) * scale
        key_terms = jnp.einsum('aqjk,aqd->ajkd', dscores, query_part) * scale
        value_terms = jnp.einsum('aqjk,aqd->ajkd', probs_b, grad_part)
        key_total = sum(jnp.pad(key_terms[:, offset], ((offset, span - 1 - offset), (0, 0), (0, 0))) for offset in range(span))
        value_total = sum(jnp.pad(value_terms[:, offset], ((offset, span - 1 - offset), (0, 0), (0, 0))) for offset in range(span))
        grad_key = key_total[RADIUS:RADIUS + FRAMES]
        grad_value = value_total[RADIUS:RADIUS + FRAMES]
        return (grad_query.reshape(TOKENS, HD).astype(jnp.bfloat16),
                grad_key.reshape(TOKENS, HD).astype(jnp.bfloat16),
                grad_value.reshape(TOKENS, HD).astype(jnp.bfloat16))

    grad_q, grad_k, grad_v = lax.map(one_head, jnp.arange(HEADS, dtype=jnp.int32))

    def arrange(stacked):
        return jnp.transpose(stacked, (1, 0, 2)).reshape(TOKENS, HEADS * HD)

    return (arrange(grad_q), arrange(grad_k), arrange(grad_v))
```

```python
import functools
import math

import jax
import jax.numpy as jnp
from jax import lax
from jax.experimental import pallas as pl
from jax.experimental.pallas import tpu as pltpu
from jax.sharding import PartitionSpec as P

FRAME = 256
RADIUS = 2
RIM = RADIUS * FRAME
GROUP = 1
VMEM = 48 * 1024 * 1024


def dot(a, b, contract):
    return lax.dot_general(a, b, (contract, ((), ())), preferred_element_type=jnp.float32)


def grads_kernel(
    base, radius, clips, first, q_ref, k_ref, v_ref, g_ref, before, after, *rest
):
    gq_ref, gk_ref, gv_ref, up_ref, down_ref, k_ext, v_ext, k_turned, dk, dv = rest[-10:]
    rows, width = q_ref.shape
    count = rows // FRAME
    scale = width ** (-0.5)
    factor = scale * math.log2(math.e)
    reach = radius[base + pl.program_id(0)]
    total = clips.shape[0]

    for ext, own, part in ((k_ext, k_ref, 0), (v_ext, v_ref, 1)):
        ext[0:RIM, :] = before[part]
        ext[RIM : RIM + rows, :] = own[...]
        ext[RIM + rows :, :] = after[part]
    k_turned[...] = k_ext[...].T
    dk[...] = jnp.zeros_like(dk)
    dv[...] = jnp.zeros_like(dv)

    def work(frame, low, tiles):
        span = tiles * FRAME
        mine = pl.ds(pl.multiple_of(frame * FRAME, FRAME), FRAME)
        window = pl.ds(pl.multiple_of(low * FRAME, FRAME), span)
        q = q_ref[mine, :]
        g = g_ref[mine, :]
        scores = dot(k_ext[window, :], q, ((1,), (1,)))
        dprobs = dot(v_ext[window, :], g, ((1,), (1,)))
        highest = jnp.max(scores, axis=0, keepdims=True)
        expo = jnp.exp2((scores - highest) * factor)
        probs = expo * (1.0 / jnp.sum(expo, axis=0, keepdims=True))
        dv[window, :] += dot(probs.astype(jnp.bfloat16), g, ((1,), (0,)))
        delta = jnp.sum(probs * dprobs, axis=0, keepdims=True)
        dscores = (probs * (dprobs - delta)).astype(jnp.bfloat16)
        dk[window, :] += dot(dscores, q, ((1,), (0,)))
        turned = dot(k_turned[:, window], dscores, ((1,), (0,)))
        gq_ref[mine, :] = (turned.T * scale).astype(jnp.bfloat16)

    def each(frame, carry):
        place = first[0] + frame
        clip = clips[place]
        left = jnp.int32(0)
        right = jnp.int32(0)
        for step in range(1, RADIUS + 1):
            other = jnp.maximum(place - step, 0)
            ok = (step <= reach) & (place >= step) & (clips[other] == clip)
            left += ok.astype(jnp.int32)
            other = jnp.minimum(place + step, total - 1)
            ok = (step <= reach) & (place + step < total) & (clips[other] == clip)
            right += ok.astype(jnp.int32)
        number = left + right + 1
        low = frame + RADIUS - left
        for tiles in range(1, 2 * RADIUS + 2):
            pl.when(number == tiles)(functools.partial(work, frame, low, tiles))
        return carry

    lax.fori_loop(0, count, each, 0)
    gk_ref[...] = (dk[RIM : RIM + rows, :] * scale).astype(jnp.bfloat16)
    gv_ref[...] = dv[RIM : RIM + rows, :].astype(jnp.bfloat16)
    up_ref[0] = (dk[:RIM, :] * scale).astype(jnp.bfloat16)
    up_ref[1] = dv[:RIM, :].astype(jnp.bfloat16)
    down_ref[0] = (dk[RIM + rows :, :] * scale).astype(jnp.bfloat16)
    down_ref[1] = dv[RIM + rows :, :].astype(jnp.bfloat16)


def group_grads(base, size, radius, clips, first, q, k, v, g, before, after, prior):
    rows, columns = q.shape
    width = columns // radius.shape[0]
    ext = rows + 2 * RIM
    whole = pl.BlockSpec((rows, width), lambda h, *_: (0, base + h))
    local = pl.BlockSpec((rows, width), lambda h, *_: (0, h))
    rim = pl.BlockSpec((2, RIM, width), lambda h, *_: (0, 0, base + h))
    rim_out = pl.BlockSpec((2, RIM, width), lambda h, *_: (0, 0, h))
    full = jax.ShapeDtypeStruct((rows, columns), jnp.bfloat16)
    edge = jax.ShapeDtypeStruct((2, RIM, size * width), jnp.bfloat16)
    return pl.pallas_call(
        functools.partial(grads_kernel, base),
        out_shape=[full, full, full, edge, edge],
        grid_spec=pltpu.PrefetchScalarGridSpec(
            num_scalar_prefetch=3,
            grid=(size,),
            in_specs=[whole, whole, whole, local, rim, rim]
            + [pl.BlockSpec(memory_space=pl.ANY)] * len(prior),
            out_specs=[whole, whole, whole, rim_out, rim_out],
            scratch_shapes=[
                pltpu.VMEM((ext, width), jnp.bfloat16),
                pltpu.VMEM((ext, width), jnp.bfloat16),
                pltpu.VMEM((width, ext), jnp.bfloat16),
                pltpu.VMEM((ext, width), jnp.float32),
                pltpu.VMEM((ext, width), jnp.float32),
            ],
        ),
        input_output_aliases={9 + i: i for i in range(len(prior))},
        cost_estimate=pl.CostEstimate(
            flops=size * rows * RIM * 5 * 5 * width,
            bytes_accessed=size * rows * width * 16,
            transcendentals=size * rows * RIM * 2,
        ),
        compiler_params=pltpu.CompilerParams(vmem_limit_bytes=VMEM),
    )(radius, clips, first, q, k, v, g, before, after, *prior)


def add_kernel(parts, gk_ref, gv_ref, *rest):
    received, (ok_ref, ov_ref) = rest[: 2 * parts], rest[2 * parts :]

    def add(refs):
        for index, ref in enumerate(refs):
            wide = ref.shape[2]
            columns = slice(index * wide, (index + 1) * wide)
            for part, own, out in ((0, gk_ref, ok_ref), (1, gv_ref, ov_ref)):
                total = own[:, columns].astype(jnp.float32) + ref[part].astype(jnp.float32)
                out[:, columns] = total.astype(jnp.bfloat16)

    pl.when(pl.program_id(0) == 0)(lambda: add(received[:parts]))
    pl.when(pl.program_id(0) == 1)(lambda: add(received[parts:]))


def add_rims(gk, gv, from_previous, from_next):
    rows, columns = gk.shape
    parts = len(from_previous)
    last = rows // RIM - 1
    own = pl.BlockSpec((RIM, columns), lambda i: (i * last, 0))
    received = [pl.BlockSpec(a.shape, lambda i: (0, 0, 0)) for a in from_previous + from_next]
    shape = jax.ShapeDtypeStruct(gk.shape, gk.dtype)
    return pl.pallas_call(
        functools.partial(add_kernel, parts),
        out_shape=[shape, shape],
        grid=(2,),
        in_specs=[own, own] + received,
        out_specs=[own, own],
        input_output_aliases={0: 0, 1: 1},
        compiler_params=pltpu.CompilerParams(vmem_limit_bytes=VMEM),
    )(gk, gv, *from_previous, *from_next)


def per_device(queries, saved_keys, saved_values, out_grad, radius, clip_ids):
    heads = radius.shape[0]
    rows, columns = queries.shape
    width = columns // heads
    ranks = lax.axis_size("head")
    size = lax.axis_size("tm")
    ahead = [(i, i + 1) for i in range(size - 1)]
    back = [(i + 1, i) for i in range(size - 1)]
    group = GROUP if heads % GROUP == 0 else heads
    groups = heads // group

    own_rows = out_grad.shape[0]
    cut = out_grad.reshape(own_rows, ranks, groups, group * width)
    grads = []
    for index in range(groups):
        piece = jnp.transpose(cut[:, :, index], (1, 0, 2))
        piece = lax.all_to_all(piece, "head", split_axis=0, concat_axis=0, tiled=True)
        grads.append(piece.reshape(rows, group * width))
    lasts = jnp.stack([saved_keys[rows - RIM :], saved_values[rows - RIM :]], 0)
    firsts = jnp.stack([saved_keys[:RIM], saved_values[:RIM]], 0)
    before = lax.ppermute(lasts, "tm", ahead)
    after = lax.ppermute(firsts, "tm", back)
    first = (lax.axis_index("tm") * (rows // FRAME)).astype(jnp.int32).reshape(1)

    prior, ups, downs = (), [], []
    for index in range(groups):
        *prior, up, down = group_grads(
            index * group, group, radius, clip_ids, first, queries, saved_keys, saved_values,
            grads[index], before, after, prior,
        )
        ups.append(lax.ppermute(up, "tm", back))
        downs.append(lax.ppermute(down, "tm", ahead))
    gq, gk, gv = prior
    gk, gv = add_rims(gk, gv, downs, ups)
    return gq, gk, gv


def solution(mesh):
    placed = (
        P("tm", "head"),
        P("tm", "head"),
        P("tm", "head"),
        P(("tm", "head"), None),
        P("head"),
        P(),
    )
    return jax.shard_map(
        per_device,
        mesh=mesh,
        in_specs=placed,
        out_specs=(P("tm", "head"), P("tm", "head"), P("tm", "head")),
        check_vma=False,
    )
```

```python
import functools
import math

import jax
import jax.numpy as jnp
from jax import lax
from jax.experimental import pallas as pl
from jax.experimental.pallas import tpu as pltpu
from jax.sharding import PartitionSpec as P

FRAME = 256
RADIUS = 2
RIM = RADIUS * FRAME
GROUP = 2
MESH = pl.DeviceIdType.MESH
VMEM = 48 * 1024 * 1024


def dot(a, b, contract):
    return lax.dot_general(a, b, (contract, ((), ())), preferred_element_type=jnp.float32)


def grads_kernel(
    base, radius, clips, first, q_ref, k_ref, v_ref, g_ref, before, after, *rest
):
    gq_ref, gk_ref, gv_ref, up_ref, down_ref, k_ext, v_ext, k_turned, dk, dv = rest[-10:]
    rows, width = q_ref.shape
    count = rows // FRAME
    scale = width ** (-0.5)
    factor = scale * math.log2(math.e)
    reach = radius[base + pl.program_id(0)]
    total = clips.shape[0]

    for ext, own, part in ((k_ext, k_ref, 0), (v_ext, v_ref, 1)):
        ext[0:RIM, :] = before[part]
        ext[RIM : RIM + rows, :] = own[...]
        ext[RIM + rows :, :] = after[part]
    k_turned[...] = k_ext[...].T
    dk[...] = jnp.zeros_like(dk)
    dv[...] = jnp.zeros_like(dv)

    def work(frame, low, tiles):
        span = tiles * FRAME
        mine = pl.ds(pl.multiple_of(frame * FRAME, FRAME), FRAME)
        window = pl.ds(pl.multiple_of(low * FRAME, FRAME), span)
        q = q_ref[mine, :]
        g = g_ref[mine, :]
        scores = dot(k_ext[window, :], q, ((1,), (1,)))
        dprobs = dot(v_ext[window, :], g, ((1,), (1,)))
        highest = jnp.max(scores, axis=0, keepdims=True)
        expo = jnp.exp2((scores - highest) * factor)
        probs = expo * (1.0 / jnp.sum(expo, axis=0, keepdims=True))
        dv[window, :] += dot(probs.astype(jnp.bfloat16), g, ((1,), (0,)))
        delta = jnp.sum(probs * dprobs, axis=0, keepdims=True)
        dscores = (probs * (dprobs - delta)).astype(jnp.bfloat16)
        dk[window, :] += dot(dscores, q, ((1,), (0,)))
        turned = dot(k_turned[:, window], dscores, ((1,), (0,)))
        gq_ref[mine, :] = (turned.T * scale).astype(jnp.bfloat16)

    def each(frame, carry):
        place = first[0] + frame
        clip = clips[place]
        left = jnp.int32(0)
        right = jnp.int32(0)
        for step in range(1, RADIUS + 1):
            other = jnp.maximum(place - step, 0)
            ok = (step <= reach) & (place >= step) & (clips[other] == clip)
            left += ok.astype(jnp.int32)
            other = jnp.minimum(place + step, total - 1)
            ok = (step <= reach) & (place + step < total) & (clips[other] == clip)
            right += ok.astype(jnp.int32)
        number = left + right + 1
        low = frame + RADIUS - left
        for tiles in range(1, 2 * RADIUS + 2):
            pl.when(number == tiles)(functools.partial(work, frame, low, tiles))
        return carry

    lax.fori_loop(0, count, each, 0)
    gk_ref[...] = (dk[RIM : RIM + rows, :] * scale).astype(jnp.bfloat16)
    gv_ref[...] = dv[RIM : RIM + rows, :].astype(jnp.bfloat16)
    up_ref[0] = (dk[:RIM, :] * scale).astype(jnp.bfloat16)
    up_ref[1] = dv[:RIM, :].astype(jnp.bfloat16)
    down_ref[0] = (dk[RIM + rows :, :] * scale).astype(jnp.bfloat16)
    down_ref[1] = dv[RIM + rows :, :].astype(jnp.bfloat16)


def group_grads(base, size, radius, clips, first, q, k, v, g, before, after, prior):
    rows, columns = q.shape
    width = columns // radius.shape[0]
    ext = rows + 2 * RIM
    whole = pl.BlockSpec((rows, width), lambda h, *_: (0, base + h))
    rim = pl.BlockSpec((2, RIM, width), lambda h, *_: (0, 0, base + h))
    rim_out = pl.BlockSpec((2, RIM, width), lambda h, *_: (0, 0, h))
    full = jax.ShapeDtypeStruct((rows, columns), jnp.bfloat16)
    edge = jax.ShapeDtypeStruct((2, RIM, size * width), jnp.bfloat16)
    return pl.pallas_call(
        functools.partial(grads_kernel, base),
        out_shape=[full, full, full, edge, edge],
        grid_spec=pltpu.PrefetchScalarGridSpec(
            num_scalar_prefetch=3,
            grid=(size,),
            in_specs=[whole, whole, whole, whole, rim, rim]
            + [pl.BlockSpec(memory_space=pl.ANY)] * len(prior),
            out_specs=[whole, whole, whole, rim_out, rim_out],
            scratch_shapes=[
                pltpu.VMEM((ext, width), jnp.bfloat16),
                pltpu.VMEM((ext, width), jnp.bfloat16),
                pltpu.VMEM((width, ext), jnp.bfloat16),
                pltpu.VMEM((ext, width), jnp.float32),
                pltpu.VMEM((ext, width), jnp.float32),
            ],
        ),
        input_output_aliases={9 + i: i for i in range(len(prior))},
        cost_estimate=pl.CostEstimate(
            flops=4 * size * rows * RIM * 5 * 5 * width,
            bytes_accessed=size * rows * width * 16,
            transcendentals=size * rows * RIM * 2,
        ),
        compiler_params=pltpu.CompilerParams(vmem_limit_bytes=VMEM),
    )(radius, clips, first, q, k, v, g, before, after, *prior)


def exchange_kernel(
    ranks, size, g_ref, k_ref, v_ref, out_ref, before, after,
    own_sem, send_sem, recv_sem, rim_send, rim_recv,
):
    me, stage = lax.axis_index("head"), lax.axis_index("tm")
    share, rows, columns = g_ref.shape[0], k_ref.shape[0], k_ref.shape[1]
    has_last, has_next = stage > 0, stage < size - 1

    barrier = pltpu.get_barrier_semaphore()

    def greet(step, carry):
        partner = lax.rem(me + step, ranks)
        pl.semaphore_signal(barrier, inc=1, device_id=(stage, partner), device_id_type=MESH)
        return carry

    lax.fori_loop(1, ranks, greet, 0)

    @pl.when(has_last)
    def _():
        pl.semaphore_signal(barrier, inc=1, device_id=(stage - 1, me), device_id_type=MESH)

    @pl.when(has_next)
    def _():
        pl.semaphore_signal(barrier, inc=1, device_id=(stage + 1, me), device_id_type=MESH)

    beside = has_last.astype(jnp.int32) + has_next.astype(jnp.int32)
    pl.semaphore_wait(barrier, ranks - 1 + beside)

    def rim(slot, source, target, to):
        return pltpu.make_async_remote_copy(
            src_ref=source,
            dst_ref=target,
            send_sem=rim_send.at[slot],
            recv_sem=rim_recv.at[slot],
            device_id=(to, me),
            device_id_type=MESH,
        )

    def forward():
        tail = pl.ds(rows - RIM, RIM)
        return (
            rim(0, k_ref.at[tail, :], before.at[0], stage + 1),
            rim(1, v_ref.at[tail, :], before.at[1], stage + 1),
        )

    def backward():
        head = pl.ds(0, RIM)
        return (
            rim(2, k_ref.at[head, :], after.at[0], stage - 1),
            rim(3, v_ref.at[head, :], after.at[1], stage - 1),
        )

    @pl.when(has_next)
    def _():
        for copy in forward():
            copy.start()

    @pl.when(has_last)
    def _():
        for copy in backward():
            copy.start()

    def place(rank):
        return pl.ds(pl.multiple_of(rank * share, share), share)

    def taken(rank):
        return pl.ds(pl.multiple_of(rank * columns, columns), columns)

    def block(step):
        partner = lax.rem(me + step, ranks)
        return pltpu.make_async_remote_copy(
            src_ref=g_ref.at[:, taken(partner)],
            dst_ref=out_ref.at[place(me), :],
            send_sem=send_sem.at[step],
            recv_sem=recv_sem.at[step],
            device_id=(stage, partner),
            device_id_type=MESH,
        )

    def begin(step, carry):
        block(step).start()
        return carry

    lax.fori_loop(1, ranks, begin, 0)
    own = pltpu.make_async_copy(g_ref.at[:, taken(me)], out_ref.at[place(me), :], own_sem)
    own.start()
    own.wait()

    def finish(step, carry):
        block(step).wait()
        return carry

    lax.fori_loop(1, ranks, finish, 0)

    @pl.when(has_next)
    def _():
        for copy in forward():
            copy.wait_send()
        for slot in (2, 3):
            rim(slot, k_ref.at[pl.ds(0, RIM), :], after.at[slot - 2], stage + 1).wait_recv()

    @pl.when(has_last)
    def _():
        for copy in backward():
            copy.wait_send()
        for slot in (0, 1):
            rim(slot, k_ref.at[pl.ds(0, RIM), :], before.at[slot], stage - 1).wait_recv()


def exchange(out_grad, keys, values, ranks, size):
    columns = keys.shape[1]
    edge = jax.ShapeDtypeStruct((2, RIM, columns), keys.dtype)
    dma = pltpu.SemaphoreType.DMA
    return pl.pallas_call(
        functools.partial(exchange_kernel, ranks, size),
        out_shape=[jax.ShapeDtypeStruct(keys.shape, out_grad.dtype), edge, edge],
        in_specs=[pl.BlockSpec(memory_space=pl.ANY)] * 3,
        out_specs=[pl.BlockSpec(memory_space=pl.ANY)] * 3,
        scratch_shapes=[dma, dma((ranks,)), dma((ranks,)), dma((4,)), dma((4,))],
        compiler_params=pltpu.CompilerParams(collective_id=0, has_side_effects=True),
    )(out_grad, keys, values)


def add_kernel(parts, gk_ref, gv_ref, *rest):
    received, (ok_ref, ov_ref) = rest[: 2 * parts], rest[2 * parts :]

    def add(refs):
        for index, ref in enumerate(refs):
            wide = ref.shape[2]
            columns = slice(index * wide, (index + 1) * wide)
            for part, own, out in ((0, gk_ref, ok_ref), (1, gv_ref, ov_ref)):
                total = own[:, columns].astype(jnp.float32) + ref[part].astype(jnp.float32)
                out[:, columns] = total.astype(jnp.bfloat16)

    pl.when(pl.program_id(0) == 0)(lambda: add(received[:parts]))
    pl.when(pl.program_id(0) == 1)(lambda: add(received[parts:]))


def add_rims(gk, gv, from_previous, from_next):
    rows, columns = gk.shape
    parts = len(from_previous)
    last = rows // RIM - 1
    own = pl.BlockSpec((RIM, columns), lambda i: (i * last, 0))
    received = [pl.BlockSpec(a.shape, lambda i: (0, 0, 0)) for a in from_previous + from_next]
    shape = jax.ShapeDtypeStruct(gk.shape, gk.dtype)
    return pl.pallas_call(
        functools.partial(add_kernel, parts),
        out_shape=[shape, shape],
        grid=(2,),
        in_specs=[own, own] + received,
        out_specs=[own, own],
        input_output_aliases={0: 0, 1: 1},
        compiler_params=pltpu.CompilerParams(vmem_limit_bytes=VMEM),
    )(gk, gv, *from_previous, *from_next)


def per_device(queries, saved_keys, saved_values, out_grad, radius, clip_ids):
    heads = radius.shape[0]
    rows, columns = queries.shape
    width = columns // heads
    ranks = lax.axis_size("head")
    size = lax.axis_size("tm")
    ahead = [(i, i + 1) for i in range(size - 1)]
    back = [(i + 1, i) for i in range(size - 1)]
    group = GROUP if heads % GROUP == 0 else heads
    groups = heads // group

    grads, before, after = exchange(out_grad, saved_keys, saved_values, ranks, size)
    first = (lax.axis_index("tm") * (rows // FRAME)).astype(jnp.int32).reshape(1)

    prior, ups, downs = (), [], []
    for index in range(groups):
        *prior, up, down = group_grads(
            index * group, group, radius, clip_ids, first, queries, saved_keys, saved_values,
            grads, before, after, prior,
        )
        ups.append(lax.ppermute(up, "tm", back))
        downs.append(lax.ppermute(down, "tm", ahead))
    gq, gk, gv = prior
    gk, gv = add_rims(gk, gv, downs, ups)
    return gq, gk, gv


def solution(mesh):
    placed = (
        P("tm", "head"),
        P("tm", "head"),
        P("tm", "head"),
        P(("tm", "head"), None),
        P("head"),
        P(),
    )
    return jax.shard_map(
        per_device,
        mesh=mesh,
        in_specs=placed,
        out_specs=(P("tm", "head"), P("tm", "head"), P("tm", "head")),
        check_vma=False,
    )
```

```python
import functools
import math

import jax
import jax.numpy as jnp
from jax import lax
from jax.experimental import pallas as pl
from jax.experimental.pallas import tpu as pltpu
from jax.sharding import PartitionSpec as P

FRAME = 256
RADIUS = 2
RIM = RADIUS * FRAME
MESH = pl.DeviceIdType.MESH
VMEM = 48 * 1024 * 1024


def dot(a, b, contract):
    return lax.dot_general(a, b, (contract, ((), ())), preferred_element_type=jnp.float32)


def grads_kernel(outer, radius, clips, first, q_ref, k_ref, v_ref, g_ref, *rest):
    rows, width = q_ref.shape
    count = rows // FRAME
    scale = width ** (-0.5)
    factor = scale * math.log2(math.e)
    reach = radius[pl.program_id(0)]
    total = clips.shape[0]

    if outer:
        before, after, gq_ref, gk_ref, gv_ref, up_ref, down_ref = rest[:7]
        k_all, v_all, k_turned, dk, dv = rest[7:]
        for ext, own, part in ((k_all, k_ref, 0), (v_all, v_ref, 1)):
            ext[0:RIM, :] = before[part]
            ext[RIM : RIM + rows, :] = own[...]
            ext[RIM + rows :, :] = after[part]
    else:
        gq_old, gk_old, gv_old, gq_ref, gk_ref, gv_ref, k_turned, dk, dv = rest
        k_all, v_all = k_ref, v_ref
        gq_ref[...] = gq_old[...]
    k_turned[...] = k_all[...].T
    dk[...] = jnp.zeros_like(dk)
    dv[...] = jnp.zeros_like(dv)

    def work(frame, low, tiles):
        span = tiles * FRAME
        mine = pl.ds(pl.multiple_of(frame * FRAME, FRAME), FRAME)
        window = pl.ds(pl.multiple_of(low * FRAME, FRAME), span)
        q = q_ref[mine, :]
        g = g_ref[mine, :]
        scores = dot(k_all[window, :], q, ((1,), (1,)))
        dprobs = dot(v_all[window, :], g, ((1,), (1,)))
        highest = jnp.max(scores, axis=0, keepdims=True)
        expo = jnp.exp2((scores - highest) * factor)
        probs = expo * (1.0 / jnp.sum(expo, axis=0, keepdims=True))
        dv[window, :] += dot(probs.astype(jnp.bfloat16), g, ((1,), (0,)))
        delta = jnp.sum(probs * dprobs, axis=0, keepdims=True)
        dscores = (probs * (dprobs - delta)).astype(jnp.bfloat16)
        dk[window, :] += dot(dscores, q, ((1,), (0,)))
        turned = dot(k_turned[:, window], dscores, ((1,), (0,)))
        gq_ref[mine, :] = (turned.T * scale).astype(jnp.bfloat16)

    def each(index, carry):
        if outer:
            frame = index + (index >= RADIUS).astype(jnp.int32) * (count - 2 * RADIUS)
        else:
            frame = index + RADIUS
        place = first[0] + frame
        clip = clips[place]
        left = jnp.int32(0)
        right = jnp.int32(0)
        for step in range(1, RADIUS + 1):
            other = jnp.maximum(place - step, 0)
            ok = (step <= reach) & (place >= step) & (clips[other] == clip)
            left += ok.astype(jnp.int32)
            other = jnp.minimum(place + step, total - 1)
            ok = (step <= reach) & (place + step < total) & (clips[other] == clip)
            right += ok.astype(jnp.int32)
        number = left + right + 1
        low = frame + (RADIUS if outer else 0) - left
        for tiles in range(1, 2 * RADIUS + 2):
            pl.when(number == tiles)(functools.partial(work, frame, low, tiles))
        return carry

    lax.fori_loop(0, 2 * RADIUS if outer else count - 2 * RADIUS, each, 0)
    if outer:
        gk_ref[...] = (dk[RIM : RIM + rows, :] * scale).astype(jnp.bfloat16)
        gv_ref[...] = dv[RIM : RIM + rows, :].astype(jnp.bfloat16)
        up_ref[0] = (dk[:RIM, :] * scale).astype(jnp.bfloat16)
        up_ref[1] = dv[:RIM, :].astype(jnp.bfloat16)
        down_ref[0] = (dk[RIM + rows :, :] * scale).astype(jnp.bfloat16)
        down_ref[1] = dv[RIM + rows :, :].astype(jnp.bfloat16)
    else:
        gk_ref[...] = (dk[...] * scale + gk_old[...].astype(jnp.float32)).astype(jnp.bfloat16)
        gv_ref[...] = (dv[...] + gv_old[...].astype(jnp.float32)).astype(jnp.bfloat16)


def part_grads(radius, clips, first, q, k, v, g, rims=(), prior=()):
    rows, columns = q.shape
    heads = radius.shape[0]
    width = columns // heads
    outer = not prior
    ext = rows + (2 * RIM if outer else 0)
    whole = pl.BlockSpec((rows, width), lambda h, *_: (0, h))
    rim = pl.BlockSpec((2, RIM, width), lambda h, *_: (0, 0, h))
    full = jax.ShapeDtypeStruct((rows, columns), jnp.bfloat16)
    edge = jax.ShapeDtypeStruct((2, RIM, columns), jnp.bfloat16)
    edges = 2 if outer else 0
    work = heads * (2 * RIM if outer else rows - 2 * RIM) * RIM * 5 * width
    return pl.pallas_call(
        functools.partial(grads_kernel, outer),
        out_shape=[full] * 3 + [edge] * edges,
        grid_spec=pltpu.PrefetchScalarGridSpec(
            num_scalar_prefetch=3,
            grid=(heads,),
            in_specs=[whole] * 4 + [rim] * len(rims) + [whole] * len(prior),
            out_specs=[whole] * 3 + [rim] * edges,
            scratch_shapes=[pltpu.VMEM((ext, width), jnp.bfloat16)] * edges
            + [
                pltpu.VMEM((width, ext), jnp.bfloat16),
                pltpu.VMEM((ext, width), jnp.float32),
                pltpu.VMEM((ext, width), jnp.float32),
            ],
        ),
        input_output_aliases={7 + i: i for i in range(len(prior))},
        cost_estimate=pl.CostEstimate(
            flops=20 * work, bytes_accessed=heads * rows * width * 16, transcendentals=work // width
        ),
        compiler_params=pltpu.CompilerParams(vmem_limit_bytes=VMEM),
    )(radius, clips, first, q, k, v, g, *rims, *prior)


def exchange_kernel(
    ranks, size, g_ref, k_ref, v_ref, out_ref, before, after,
    own_sem, send_sem, recv_sem, rim_send, rim_recv,
):
    me, stage = lax.axis_index("head"), lax.axis_index("tm")
    share, rows, columns = g_ref.shape[0], k_ref.shape[0], k_ref.shape[1]
    has_last, has_next = stage > 0, stage < size - 1

    barrier = pltpu.get_barrier_semaphore()

    def greet(step, carry):
        partner = lax.rem(me + step, ranks)
        pl.semaphore_signal(barrier, inc=1, device_id=(stage, partner), device_id_type=MESH)
        return carry

    lax.fori_loop(1, ranks, greet, 0)

    @pl.when(has_last)
    def _():
        pl.semaphore_signal(barrier, inc=1, device_id=(stage - 1, me), device_id_type=MESH)

    @pl.when(has_next)
    def _():
        pl.semaphore_signal(barrier, inc=1, device_id=(stage + 1, me), device_id_type=MESH)

    beside = has_last.astype(jnp.int32) + has_next.astype(jnp.int32)
    pl.semaphore_wait(barrier, ranks - 1 + beside)

    def rim(slot, source, target, to):
        return pltpu.make_async_remote_copy(
            src_ref=source,
            dst_ref=target,
            send_sem=rim_send.at[slot],
            recv_sem=rim_recv.at[slot],
            device_id=(to, me),
            device_id_type=MESH,
        )

    def forward():
        tail = pl.ds(rows - RIM, RIM)
        return (
            rim(0, k_ref.at[tail, :], before.at[0], stage + 1),
            rim(1, v_ref.at[tail, :], before.at[1], stage + 1),
        )

    def backward():
        head = pl.ds(0, RIM)
        return (
            rim(2, k_ref.at[head, :], after.at[0], stage - 1),
            rim(3, v_ref.at[head, :], after.at[1], stage - 1),
        )

    @pl.when(has_next)
    def _():
        for copy in forward():
            copy.start()

    @pl.when(has_last)
    def _():
        for copy in backward():
            copy.start()

    def place(rank):
        return pl.ds(pl.multiple_of(rank * share, share), share)

    def taken(rank):
        return pl.ds(pl.multiple_of(rank * columns, columns), columns)

    def block(step):
        partner = lax.rem(me + step, ranks)
        return pltpu.make_async_remote_copy(
            src_ref=g_ref.at[:, taken(partner)],
            dst_ref=out_ref.at[place(me), :],
            send_sem=send_sem.at[step],
            recv_sem=recv_sem.at[step],
            device_id=(stage, partner),
            device_id_type=MESH,
        )

    def begin(step, carry):
        block(step).start()
        return carry

    lax.fori_loop(1, ranks, begin, 0)
    own = pltpu.make_async_copy(g_ref.at[:, taken(me)], out_ref.at[place(me), :], own_sem)
    own.start()
    own.wait()

    def finish(step, carry):
        block(step).wait()
        return carry

    lax.fori_loop(1, ranks, finish, 0)

    @pl.when(has_next)
    def _():
        for copy in forward():
            copy.wait_send()
        for slot in (2, 3):
            rim(slot, k_ref.at[pl.ds(0, RIM), :], after.at[slot - 2], stage + 1).wait_recv()

    @pl.when(has_last)
    def _():
        for copy in backward():
            copy.wait_send()
        for slot in (0, 1):
            rim(slot, k_ref.at[pl.ds(0, RIM), :], before.at[slot], stage - 1).wait_recv()


def exchange(out_grad, keys, values, ranks, size):
    columns = keys.shape[1]
    edge = jax.ShapeDtypeStruct((2, RIM, columns), keys.dtype)
    dma = pltpu.SemaphoreType.DMA
    return pl.pallas_call(
        functools.partial(exchange_kernel, ranks, size),
        out_shape=[jax.ShapeDtypeStruct(keys.shape, out_grad.dtype), edge, edge],
        in_specs=[pl.BlockSpec(memory_space=pl.ANY)] * 3,
        out_specs=[pl.BlockSpec(memory_space=pl.ANY)] * 3,
        scratch_shapes=[dma, dma((ranks,)), dma((ranks,)), dma((4,)), dma((4,))],
        compiler_params=pltpu.CompilerParams(collective_id=0, has_side_effects=True),
    )(out_grad, keys, values)


def add_kernel(parts, gk_ref, gv_ref, *rest):
    received, (ok_ref, ov_ref) = rest[: 2 * parts], rest[2 * parts :]

    def add(refs):
        for index, ref in enumerate(refs):
            wide = ref.shape[2]
            columns = slice(index * wide, (index + 1) * wide)
            for part, own, out in ((0, gk_ref, ok_ref), (1, gv_ref, ov_ref)):
                total = own[:, columns].astype(jnp.float32) + ref[part].astype(jnp.float32)
                out[:, columns] = total.astype(jnp.bfloat16)

    pl.when(pl.program_id(0) == 0)(lambda: add(received[:parts]))
    pl.when(pl.program_id(0) == 1)(lambda: add(received[parts:]))


def add_rims(gk, gv, from_previous, from_next):
    rows, columns = gk.shape
    parts = len(from_previous)
    last = rows // RIM - 1
    own = pl.BlockSpec((RIM, columns), lambda i: (i * last, 0))
    received = [pl.BlockSpec(a.shape, lambda i: (0, 0, 0)) for a in from_previous + from_next]
    shape = jax.ShapeDtypeStruct(gk.shape, gk.dtype)
    return pl.pallas_call(
        functools.partial(add_kernel, parts),
        out_shape=[shape, shape],
        grid=(2,),
        in_specs=[own, own] + received,
        out_specs=[own, own],
        input_output_aliases={0: 0, 1: 1},
        compiler_params=pltpu.CompilerParams(vmem_limit_bytes=VMEM),
    )(gk, gv, *from_previous, *from_next)


def per_device(queries, saved_keys, saved_values, out_grad, radius, clip_ids):
    rows = queries.shape[0]
    ranks = lax.axis_size("head")
    size = lax.axis_size("tm")
    ahead = [(i, i + 1) for i in range(size - 1)]
    back = [(i + 1, i) for i in range(size - 1)]
    grads, before, after = exchange(out_grad, saved_keys, saved_values, ranks, size)
    first = (lax.axis_index("tm") * (rows // FRAME)).astype(jnp.int32).reshape(1)
    common = (radius, clip_ids, first, queries, saved_keys, saved_values, grads)
    *partial, up, down = part_grads(*common, rims=(before, after))
    from_next = lax.ppermute(up, "tm", back)
    from_previous = lax.ppermute(down, "tm", ahead)
    gq, gk, gv = part_grads(*common, prior=partial)
    gk, gv = add_rims(gk, gv, [from_previous], [from_next])
    return gq, gk, gv


def solution(mesh):
    placed = (
        P("tm", "head"),
        P("tm", "head"),
        P("tm", "head"),
        P(("tm", "head"), None),
        P("head"),
        P(),
    )
    return jax.shard_map(
        per_device,
        mesh=mesh,
        in_specs=placed,
        out_specs=(P("tm", "head"), P("tm", "head"), P("tm", "head")),
        check_vma=False,
    )
```

```python
import functools
import math

import jax
import jax.numpy as jnp
from jax import lax
from jax.experimental import pallas as pl
from jax.experimental.pallas import tpu as pltpu
from jax.sharding import PartitionSpec as P

FRAME = 256
RADIUS = 2
RIM = RADIUS * FRAME
MESH = pl.DeviceIdType.MESH
VMEM = 48 * 1024 * 1024


def dot(a, b, contract):
    return lax.dot_general(a, b, (contract, ((), ())), preferred_element_type=jnp.float32)


def grads_kernel(side, radius, clips, first, q_ref, k_ref, v_ref, g_ref, *rest):
    rows, width = q_ref.shape
    count = rows // FRAME
    scale = width ** (-0.5)
    factor = scale * math.log2(math.e)
    reach = radius[pl.program_id(0)]
    total = clips.shape[0]

    pad = RIM if side == 0 else 0
    own, edge = pl.ds(pad, rows), pl.ds(0 if side == 0 else rows, RIM)
    rest = list(rest)
    rim = rest.pop(0) if side < 2 else None
    old = [rest.pop(0) for _ in range(3)] if side > 0 else None
    gq_ref, gk_ref, gv_ref = rest[:3]
    k_turned, dk, dv = rest[-3:]
    k_all, v_all = k_ref, v_ref
    if side < 2:
        edge_ref, k_all, v_all = rest[3:6]
        for ext, mine, part in ((k_all, k_ref, 0), (v_all, v_ref, 1)):
            ext[own, :] = mine[...]
            ext[edge, :] = rim[part]
    if side > 0:
        gq_ref[...] = old[0][...]
    k_turned[...] = k_all[...].T
    dk[...] = jnp.zeros_like(dk)
    dv[...] = jnp.zeros_like(dv)

    def work(frame, low, tiles):
        span = tiles * FRAME
        mine = pl.ds(pl.multiple_of(frame * FRAME, FRAME), FRAME)
        window = pl.ds(pl.multiple_of(low * FRAME, FRAME), span)
        q = q_ref[mine, :]
        g = g_ref[mine, :]
        scores = dot(k_all[window, :], q, ((1,), (1,)))
        dprobs = dot(v_all[window, :], g, ((1,), (1,)))
        highest = jnp.max(scores, axis=0, keepdims=True)
        expo = jnp.exp2((scores - highest) * factor)
        probs = expo * (1.0 / jnp.sum(expo, axis=0, keepdims=True))
        dv[window, :] += dot(probs.astype(jnp.bfloat16), g, ((1,), (0,)))
        delta = jnp.sum(probs * dprobs, axis=0, keepdims=True)
        dscores = (probs * (dprobs - delta)).astype(jnp.bfloat16)
        dk[window, :] += dot(dscores, q, ((1,), (0,)))
        turned = dot(k_turned[:, window], dscores, ((1,), (0,)))
        gq_ref[mine, :] = (turned.T * scale).astype(jnp.bfloat16)

    def each(index, carry):
        frame = index + (0, count - RADIUS, RADIUS)[side]
        place = first[0] + frame
        clip = clips[place]
        left = jnp.int32(0)
        right = jnp.int32(0)
        for step in range(1, RADIUS + 1):
            other = jnp.maximum(place - step, 0)
            ok = (step <= reach) & (place >= step) & (clips[other] == clip)
            left += ok.astype(jnp.int32)
            other = jnp.minimum(place + step, total - 1)
            ok = (step <= reach) & (place + step < total) & (clips[other] == clip)
            right += ok.astype(jnp.int32)
        number = left + right + 1
        low = frame + pad // FRAME - left
        for tiles in range(1, 2 * RADIUS + 2):
            pl.when(number == tiles)(functools.partial(work, frame, low, tiles))
        return carry

    lax.fori_loop(0, count - 2 * RADIUS if side == 2 else RADIUS, each, 0)
    gk, gv = dk[own, :] * scale, dv[own, :]
    if side > 0:
        gk += old[1][...].astype(jnp.float32)
        gv += old[2][...].astype(jnp.float32)
    gk_ref[...] = gk.astype(jnp.bfloat16)
    gv_ref[...] = gv.astype(jnp.bfloat16)
    if side < 2:
        edge_ref[0] = (dk[edge, :] * scale).astype(jnp.bfloat16)
        edge_ref[1] = dv[edge, :].astype(jnp.bfloat16)


def part_grads(side, radius, clips, first, q, k, v, g, rims=(), prior=()):
    rows, columns = q.shape
    heads = radius.shape[0]
    width = columns // heads
    ext = rows + (RIM if side < 2 else 0)
    whole = pl.BlockSpec((rows, width), lambda h, *_: (0, h))
    rim = pl.BlockSpec((2, RIM, width), lambda h, *_: (0, 0, h))
    full = jax.ShapeDtypeStruct((rows, columns), jnp.bfloat16)
    edge = jax.ShapeDtypeStruct((2, RIM, columns), jnp.bfloat16)
    edges = 1 if side < 2 else 0
    work = heads * (RIM if side < 2 else rows - 2 * RIM) * RIM * 5 * width
    return pl.pallas_call(
        functools.partial(grads_kernel, side),
        out_shape=[full] * 3 + [edge] * edges,
        grid_spec=pltpu.PrefetchScalarGridSpec(
            num_scalar_prefetch=3,
            grid=(heads,),
            in_specs=[whole] * 4 + [rim] * len(rims) + [whole] * len(prior),
            out_specs=[whole] * 3 + [rim] * edges,
            scratch_shapes=[pltpu.VMEM((ext, width), jnp.bfloat16)] * (2 * edges)
            + [
                pltpu.VMEM((width, ext), jnp.bfloat16),
                pltpu.VMEM((ext, width), jnp.float32),
                pltpu.VMEM((ext, width), jnp.float32),
            ],
        ),
        input_output_aliases={7 + len(rims) + i: i for i in range(len(prior))},
        cost_estimate=pl.CostEstimate(
            flops=2 * work, bytes_accessed=rows * width, transcendentals=0
        ),
        compiler_params=pltpu.CompilerParams(vmem_limit_bytes=VMEM),
    )(radius, clips, first, q, k, v, g, *rims, *prior)


def exchange_kernel(
    ranks, size, g_ref, k_ref, v_ref, out_ref, before, after,
    own_sem, send_sem, recv_sem, rim_send, rim_recv,
):
    me, stage = lax.axis_index("head"), lax.axis_index("tm")
    share, rows, columns = g_ref.shape[0], k_ref.shape[0], k_ref.shape[1]
    has_last, has_next = stage > 0, stage < size - 1

    barrier = pltpu.get_barrier_semaphore()

    def greet(step, carry):
        partner = lax.rem(me + step, ranks)
        pl.semaphore_signal(barrier, inc=1, device_id=(stage, partner), device_id_type=MESH)
        return carry

    lax.fori_loop(1, ranks, greet, 0)

    @pl.when(has_last)
    def _():
        pl.semaphore_signal(barrier, inc=1, device_id=(stage - 1, me), device_id_type=MESH)

    @pl.when(has_next)
    def _():
        pl.semaphore_signal(barrier, inc=1, device_id=(stage + 1, me), device_id_type=MESH)

    beside = has_last.astype(jnp.int32) + has_next.astype(jnp.int32)
    pl.semaphore_wait(barrier, ranks - 1 + beside)

    def rim(slot, source, target, to):
        return pltpu.make_async_remote_copy(
            src_ref=source,
            dst_ref=target,
            send_sem=rim_send.at[slot],
            recv_sem=rim_recv.at[slot],
            device_id=(to, me),
            device_id_type=MESH,
        )

    def forward():
        tail = pl.ds(rows - RIM, RIM)
        return (
            rim(0, k_ref.at[tail, :], before.at[0], stage + 1),
            rim(1, v_ref.at[tail, :], before.at[1], stage + 1),
        )

    def backward():
        head = pl.ds(0, RIM)
        return (
            rim(2, k_ref.at[head, :], after.at[0], stage - 1),
            rim(3, v_ref.at[head, :], after.at[1], stage - 1),
        )

    @pl.when(has_next)
    def _():
        for copy in forward():
            copy.start()

    @pl.when(has_last)
    def _():
        for copy in backward():
            copy.start()

    def place(rank):
        return pl.ds(pl.multiple_of(rank * share, share), share)

    def taken(rank):
        return pl.ds(pl.multiple_of(rank * columns, columns), columns)

    def block(step):
        partner = lax.rem(me + step, ranks)
        return pltpu.make_async_remote_copy(
            src_ref=g_ref.at[:, taken(partner)],
            dst_ref=out_ref.at[place(me), :],
            send_sem=send_sem.at[step],
            recv_sem=recv_sem.at[step],
            device_id=(stage, partner),
            device_id_type=MESH,
        )

    def begin(step, carry):
        block(step).start()
        return carry

    lax.fori_loop(1, ranks, begin, 0)
    own = pltpu.make_async_copy(g_ref.at[:, taken(me)], out_ref.at[place(me), :], own_sem)
    own.start()
    own.wait()

    def finish(step, carry):
        block(step).wait()
        return carry

    lax.fori_loop(1, ranks, finish, 0)

    @pl.when(has_next)
    def _():
        for copy in forward():
            copy.wait_send()
        for slot in (2, 3):
            rim(slot, k_ref.at[pl.ds(0, RIM), :], after.at[slot - 2], stage + 1).wait_recv()

    @pl.when(has_last)
    def _():
        for copy in backward():
            copy.wait_send()
        for slot in (0, 1):
            rim(slot, k_ref.at[pl.ds(0, RIM), :], before.at[slot], stage - 1).wait_recv()


def exchange(out_grad, keys, values, ranks, size):
    columns = keys.shape[1]
    edge = jax.ShapeDtypeStruct((2, RIM, columns), keys.dtype)
    dma = pltpu.SemaphoreType.DMA
    return pl.pallas_call(
        functools.partial(exchange_kernel, ranks, size),
        out_shape=[jax.ShapeDtypeStruct(keys.shape, out_grad.dtype), edge, edge],
        in_specs=[pl.BlockSpec(memory_space=pl.ANY)] * 3,
        out_specs=[pl.BlockSpec(memory_space=pl.ANY)] * 3,
        scratch_shapes=[dma, dma((ranks,)), dma((ranks,)), dma((4,)), dma((4,))],
        compiler_params=pltpu.CompilerParams(collective_id=0, has_side_effects=True),
    )(out_grad, keys, values)


def add_kernel(gk_ref, gv_ref, received, ok_ref, ov_ref):
    for part, own, out in ((0, gk_ref, ok_ref), (1, gv_ref, ov_ref)):
        total = own[...].astype(jnp.float32) + received[part].astype(jnp.float32)
        out[...] = total.astype(jnp.bfloat16)


def add_rim(gk, gv, received, place):
    columns = gk.shape[1]
    own = pl.BlockSpec((RIM, columns), lambda i: (place, 0))
    shape = jax.ShapeDtypeStruct(gk.shape, gk.dtype)
    return pl.pallas_call(
        add_kernel,
        out_shape=[shape, shape],
        grid=(1,),
        in_specs=[own, own, pl.BlockSpec(received.shape, lambda i: (0, 0, 0))],
        out_specs=[own, own],
        input_output_aliases={0: 0, 1: 1},
        cost_estimate=pl.CostEstimate(
            flops=RIM * columns * 2 * 10000, bytes_accessed=RIM * columns * 12, transcendentals=0
        ),
        compiler_params=pltpu.CompilerParams(vmem_limit_bytes=VMEM),
    )(gk, gv, received)


def per_device(queries, saved_keys, saved_values, out_grad, radius, clip_ids):
    rows = queries.shape[0]
    ranks = lax.axis_size("head")
    size = lax.axis_size("tm")
    ahead = [(i, i + 1) for i in range(size - 1)]
    back = [(i + 1, i) for i in range(size - 1)]
    grads, before, after = exchange(out_grad, saved_keys, saved_values, ranks, size)
    first = (lax.axis_index("tm") * (rows // FRAME)).astype(jnp.int32).reshape(1)
    common = (radius, clip_ids, first, queries, saved_keys, saved_values, grads)
    *partial, up = part_grads(0, *common, rims=(before,))
    from_next = lax.ppermute(up, "tm", back)
    *partial, down = part_grads(1, *common, rims=(after,), prior=partial)
    from_previous = lax.ppermute(down, "tm", ahead)
    gq, gk, gv = part_grads(2, *common, prior=partial)
    gk, gv = add_rim(gk, gv, from_next, rows // RIM - 1)
    gk, gv = add_rim(gk, gv, from_previous, 0)
    return gq, gk, gv


def solution(mesh):
    placed = (
        P("tm", "head"),
        P("tm", "head"),
        P("tm", "head"),
        P(("tm", "head"), None),
        P("head"),
        P(),
    )
    return jax.shard_map(
        per_device,
        mesh=mesh,
        in_specs=placed,
        out_specs=(P("tm", "head"), P("tm", "head"), P("tm", "head")),
        check_vma=False,
    )
```
